32 devices in a mesh: replica: 4 (over y, x), mp: 8 (over z, core).
Axes of the slice: x: 2, y: 2, z: 4, core: 2. Of those that a mesh axis runs over, the one named last changes fastest.
Arguments:
- row_table: float32 [16384, 128], P('mp'), may hold values from -3 to 3
- grad_history: float32 [16384, 128], P('mp'), may hold values from 0.1 to 1
- touched: int32 [4, 8, 8, 256], P('replica', 'mp'), may hold values from 0 to 2047
- lookup_slot: int32 [4, 256, 32, 2], P('replica', None, 'mp'), may hold values from 0 to 2047, as said below
- pool_counts: int32 [4, 256, 32], P('replica', None, 'mp'), may hold values from 1 to 2
- cross_down: bfloat16 [4096, 512], P('mp'), may hold values from -0.09375 to 0.09375
- cross_up: bfloat16 [4096, 512], P('mp'), may hold values from -0.25 to 0.25
- cross_bias: float32 [4096], P('mp'), may hold values from -3 to 3
- cotangent: bfloat16 [4, 256, 4096], P('replica', None, 'mp'), may hold values from -0.59765625 to 0.59765625
Outputs:
- crossed: bfloat16 [4, 256, 4096], P('replica', None, 'mp')
- new_table: float32 [16384, 128], P('mp')
- fresh_history_sums: float32 [16384, 128], P('mp')
The draws below stay inside these ranges and needn't reach their ends.
Inputs may be any that keep to these rules, and one draw needn't show every extreme that they name: For each group and each mp index m, the entries of lookup_slot over all 256 samples, the 4 features held by m and all 2 lookups are a permutation of 0 to 2047, so every owner receives exactly 256 slots from every mp index.
All inputs are finite; a program needn't handle non-finite values.
Results may differ from the reference program's by a relative error of at most 0.017.
Values may be sent and summed in bfloat16 or wider, within the bound.
A program may use at most 64 MiB of HBM per device.

```python
import math
import jax
import jax.numpy as jnp
from jax import lax

EMBED = 128
FEAT_DEV = 4
RANK = 512
HOT = 2
SAMPLES = 256
ROWS_DEV = 2048
SPARSE_FIELDS = 32
INPUT_W = 4096
CAP = 256
TABLE_ROWS = 16384
N_REPLICA = 4
N_MP = 8


def draw_lookup_slot(key, part):
    key = jax.random.fold_in(key, 7)
    key_list = jax.random.split(key, N_REPLICA * N_MP)
    orders = jax.vmap(lambda single: jax.random.permutation(single, N_MP * CAP))(key_list)
    orders = orders.reshape(N_REPLICA, N_MP, SAMPLES, FEAT_DEV, HOT)
    orders = jnp.transpose(orders, (0, 2, 1, 3, 4)).reshape(N_REPLICA, SAMPLES, N_MP * FEAT_DEV, HOT)
    return orders.astype(jnp.int32)


def touch_ends(result, own_key, least, largest):
    longest = result.shape.index(max(result.shape))
    spots = []
    for shift in (0, 1):
        where = [jax.random.randint(jax.random.fold_in(own_key, axis), (), 0, length) for axis, length in enumerate(result.shape)]
        where[longest] = (where[longest] + shift) % result.shape[longest]
        spots.append(tuple(where))
    return result.at[spots[0]].set(least).at[spots[1]].set(largest)


def block_scale(rng, extent, cuts, smallest, high):
    level = 1.0
    for dim, parts in cuts:
        steps = jax.random.uniform(jax.random.fold_in(jax.random.fold_in(rng, 6), dim), (parts,), jnp.float32, smallest / len(cuts), high / len(cuts))
        level = level * jnp.repeat(jnp.exp(steps), extent[dim] // parts).reshape((-1,) + (1,) * (len(extent) - 1 - dim))
    return level


def noise(key, extent, deviation, limit, pieces=(), kind=jnp.bfloat16):
    values = deviation * jax.random.normal(key, extent, jnp.float32)
    if pieces:
        values = values * block_scale(key, extent, pieces, -0.22, 0.18)
    return jnp.clip(values, -limit, limit).astype(kind)


def setup_inputs(seed: int = 0) -> dict:
    key_of = jax.random.split(jax.random.key(seed), 10)
    return {
        "row_table": noise(key_of[0], (TABLE_ROWS, EMBED), 0.5, 3.0, ((0, 8),), jnp.float32),
        "grad_history": jnp.clip(jnp.exp(math.log(1.0) - 2.3025851 * jax.random.uniform(key_of[1], (TABLE_ROWS, EMBED), jnp.float32) ** block_scale(key_of[1], (TABLE_ROWS, EMBED), ((0, 8),), -0.2, 0.2)), 0.1, 1.0),
        "touched": touch_ends(jax.random.randint(key_of[2], (N_REPLICA, N_MP, N_MP, CAP), 0, ROWS_DEV), jax.random.fold_in(key_of[2], 1), 0, ROWS_DEV - 1).astype(jnp.int32),
        "lookup_slot": draw_lookup_slot(jax.random.fold_in(key_of[9], 71), 0),
        "pool_counts": touch_ends(jax.random.randint(key_of[4], (N_REPLICA, SAMPLES, SPARSE_FIELDS), 1, HOT + 1), jax.random.fold_in(key_of[4], 1), 1, HOT).astype(jnp.int32),
        "cross_down": noise(key_of[5], (INPUT_W, RANK), INPUT_W ** -0.5, 0.09375, ((0, 8),)),
        "cross_up": noise(key_of[6], (INPUT_W, RANK), RANK ** -0.5, 0.25, ((0, 8),)),
        "cross_bias": noise(key_of[7], (INPUT_W,), 0.5, 3.0, ((0, 8),), jnp.float32),
        "cotangent": noise(key_of[8], (N_REPLICA, SAMPLES, INPUT_W), 0.1, 0.59765625, ((0, 4), (2, 8))),
    }


learn_rate = 0.5
epsilon = 1e-06

def slab_sum(left, right):
    left_slab_pieces = left.astype(jnp.float32).reshape(SAMPLES, N_MP, FEAT_DEV * EMBED)
    right_slab_pieces = right.astype(jnp.float32).reshape(N_MP, FEAT_DEV * EMBED, RANK)
    cross_terms = jnp.einsum('ujg,jgf->juf', left_slab_pieces, right_slab_pieces)
    rounded = lax.optimization_barrier(cross_terms.astype(jnp.bfloat16))
    return lax.optimization_barrier(jnp.sum(rounded.astype(jnp.float32), axis=0))

def reference(row_table, grad_history, touched, lookup_slot, pool_counts, cross_down, cross_up, cross_bias, cotangent):
    table_half = row_table.astype(jnp.bfloat16)
    asker = (jnp.arange(SPARSE_FIELDS, dtype=jnp.int32) // FEAT_DEV)[None, :, None]

    def one_group(summed, inputs):
        wanted, slot_index, counts, upstream_half = inputs
        owner = slot_index // CAP
        slot_position = slot_index % CAP
        global_row = owner * ROWS_DEV + wanted[owner, asker, slot_position]
        picked = table_half[global_row].astype(jnp.float32)
        live_mask = (jnp.arange(HOT, dtype=jnp.int32)[None, None, :] < counts[:, :, None]).astype(jnp.float32)
        divisor = counts.astype(jnp.float32)[:, :, None]
        pooled = (lax.optimization_barrier(jnp.sum(picked * live_mask[..., None], axis=2)) / divisor).astype(jnp.bfloat16)
        pooled = pooled.reshape(SAMPLES, INPUT_W)
        rounded_low = slab_sum(pooled, cross_down).astype(jnp.bfloat16)
        scaled = jnp.dot(rounded_low, cross_up.T, preferred_element_type=jnp.float32) + cross_bias[None, :]
        pooled_wide = pooled.astype(jnp.float32)
        crossed = (pooled_wide * scaled + pooled_wide).astype(jnp.bfloat16)
        upstream = upstream_half.astype(jnp.float32)
        weighted = (upstream * pooled_wide).astype(jnp.bfloat16)
        rounded_back = slab_sum(weighted, cross_up).astype(jnp.bfloat16)
        pool_grad = upstream * scaled + upstream + jnp.dot(rounded_back, cross_down.T, preferred_element_type=jnp.float32)
        lookup_grad = (pool_grad.reshape(SAMPLES, SPARSE_FIELDS, 1, EMBED) / divisor[..., None] * live_mask[..., None]).astype(jnp.bfloat16)
        summed = summed.at[global_row.reshape(-1)].add(lookup_grad.reshape(-1, EMBED).astype(jnp.float32))
        return (summed, crossed)
    start_grad = jnp.zeros((TABLE_ROWS, EMBED), jnp.float32)
    row_grad, crossed = lax.scan(one_group, start_grad, (touched, lookup_slot, pool_counts, cotangent))
    fresh_history_sums = grad_history + row_grad * row_grad
    new_table = row_table - learn_rate * row_grad / (jnp.sqrt(fresh_history_sums) + epsilon)
    return (crossed, new_table, fresh_history_sums)
```

```python
import functools

import jax
import jax.numpy as jnp
from jax import lax
from jax.experimental import pallas as pl
from jax.experimental.pallas import tpu as pltpu
from jax.sharding import PartitionSpec as P

learn_rate = 0.5
epsilon = 1e-06
LANES = 128
bf16 = jnp.bfloat16
f32 = jnp.float32


def flip(index, distance, count):
    result = 0
    bit = 1
    while bit < count:
        result = result + bit * lax.rem(
            lax.div(jnp.int32(index), jnp.int32(bit)) + lax.div(jnp.int32(distance), jnp.int32(bit)),
            jnp.int32(2),
        )
        bit *= 2
    return result


def steps(order, body):
    if len(order) <= 8:
        for d in order:
            body(d)
    else:
        first, stride = order[0], order[1] - order[0]
        lax.fori_loop(0, len(order), lambda i, c: (body(first + stride * i), c)[1], 0)


def ones_where(mask):
    return jnp.where(mask, 1.0, 0.0).astype(bf16)


def kernel(
    n,
    nr,
    table_ref,
    wanted_ref,
    slots_ref,
    counts_ref,
    down_ref,
    up_ref,
    bias_ref,
    cot_ref,
    crossed_ref,
    grad_ref,
    table_half,
    onehot,
    rows_out,
    rows_in,
    columns,
    pick,
    place,
    owned,
    pool_sum,
    pooled_half,
    weighted,
    part,
    part_in,
    reduced,
    full,
    grad_half,
    grads_out,
    grads_in,
    row_sum,
    row_part,
    row_part_in,
    row_reduced,
    row_full,
    rows_send,
    rows_recv,
    part_send,
    part_recv,
    full_send,
    full_recv,
    grads_send,
    grads_recv,
    row_part_send,
    row_part_recv,
    row_full_send,
    row_full_recv,
):
    me = lax.axis_index("mp")
    group = lax.axis_index("replica")
    cap = wanted_ref.shape[1]
    rows, width = table_ref.shape
    samples, features = counts_ref.shape
    hot = slots_ref.shape[0] // features
    rank = down_ref.shape[1]
    piece = min(cap, LANES)
    near = list(range(1, n))
    far = near[::-1]
    group_far = list(range(nr - 1, 0, -1))

    barrier = pltpu.get_barrier_semaphore()
    for_mp = lambda d: pl.semaphore_signal(
        barrier, inc=1, device_id={"mp": flip(me, d, n)}, device_id_type=pl.DeviceIdType.MESH
    )
    for_replica = lambda e: pl.semaphore_signal(
        barrier, inc=1, device_id={"replica": flip(group, e, nr)}, device_id_type=pl.DeviceIdType.MESH
    )
    steps(far, for_mp)
    steps(group_far, for_replica)

    def to_mp(src, dst, send, recv, d):
        return pltpu.make_async_remote_copy(
            src_ref=src,
            dst_ref=dst,
            send_sem=send.at[d],
            recv_sem=recv.at[d],
            device_id={"mp": flip(me, d, n)},
            device_id_type=pl.DeviceIdType.MESH,
        )

    def to_replica(src, dst, send, recv, e):
        return pltpu.make_async_remote_copy(
            src_ref=src,
            dst_ref=dst,
            send_sem=send.at[e],
            recv_sem=recv.at[e],
            device_id={"replica": flip(group, e, nr)},
            device_id_type=pl.DeviceIdType.MESH,
        )

    rows_copy = lambda d: to_mp(rows_out.at[d], rows_in.at[d], rows_send, rows_recv, d)
    part_copy = lambda d: to_mp(
        part.at[flip(me, d, n)], part_in.at[d], part_send, part_recv, d
    )
    full_copy = lambda d: to_mp(reduced, full.at[me], full_send, full_recv, d)
    grads_copy = lambda d: to_mp(grads_out.at[d], grads_in.at[d], grads_send, grads_recv, d)
    row_part_copy = lambda e: to_replica(
        row_part.at[flip(group, e, nr)], row_part_in.at[e], row_part_send, row_part_recv, e
    )
    row_full_copy = lambda e: to_replica(
        row_reduced, row_full.at[group], row_full_send, row_full_recv, e
    )

    table_half[...] = table_ref[...].astype(bf16)
    lane = lax.broadcasted_iota(jnp.int32, (cap, LANES), 1)

    def gather(d):
        row = wanted_ref[pl.ds(flip(me, d, n), 1), :]
        column = jnp.broadcast_to(row, (LANES, cap)).T
        for j in range(rows // LANES):
            onehot[:, j * LANES : (j + 1) * LANES] = ones_where(column == lane + j * LANES)
        return jnp.dot(onehot[...], table_half[...], preferred_element_type=f32).astype(bf16)

    rows_in[0] = gather(0)
    pl.semaphore_wait(barrier, n - 1 + nr - 1)

    def send_rows(d):
        rows_out[d] = gather(d)
        rows_copy(d).start()

    steps(far, send_rows)

    for i in range(hot * features):
        columns[i] = jnp.broadcast_to(slots_ref[i : i + 1, :], (LANES, samples)).T
    piece_lane = lax.broadcasted_iota(jnp.int32, (samples, piece), 1)
    cap_row = lax.broadcasted_iota(jnp.int32, (cap, samples), 0)
    block_row = lax.broadcasted_iota(jnp.int32, (LANES, cap), 0)

    def build_pick(d):
        base = flip(me, d, n) * cap
        for f in range(features):
            for j in range(cap // piece):
                mask = None
                for k in range(hot):
                    hit = columns[k * features + f][:, :piece] - (base + j * piece) == piece_lane
                    mask = hit if mask is None else mask | hit
                pick[d, f * samples : (f + 1) * samples, j * piece : (j + 1) * piece] = ones_where(mask)

    def build_place(d):
        base = flip(me, d, n) * cap
        for f in range(features):
            mask = None
            for k in range(hot):
                i = k * features + f
                hit = slots_ref[i : i + 1, :] - base == cap_row
                mask = hit if mask is None else mask | hit
            place[d, :, f * samples : (f + 1) * samples] = ones_where(mask)

    def build_owned(d):
        row = wanted_ref[pl.ds(flip(me, d, n), 1), :]
        for j in range(rows // LANES):
            owned[d, j * LANES : (j + 1) * LANES, :] = ones_where(row == block_row + j * LANES)

    steps([0] + near, build_pick)
    pool_sum[...] = jnp.dot(pick[0], rows_in[0], preferred_element_type=f32)
    steps([0] + near, build_place)
    steps([0] + near, build_owned)

    def pool(d):
        rows_copy(d).wait_recv()
        pool_sum[...] += jnp.dot(pick[d], rows_in[d], preferred_element_type=f32)

    steps(near, pool)

    for f in range(features):
        cut = slice(f * width, (f + 1) * width)
        divisor = counts_ref[:, f : f + 1].astype(f32)
        value = (pool_sum[f * samples : (f + 1) * samples, :] / divisor).astype(bf16)
        pooled_half[:, cut] = value
        weighted[:, cut] = (cot_ref[:, cut].astype(f32) * value.astype(f32)).astype(bf16)
    low = jnp.dot(pooled_half[...], down_ref[...], preferred_element_type=f32)
    part[:, :, :rank] = low.reshape(n, samples // n, rank).astype(bf16)
    back = jnp.dot(weighted[...], up_ref[...], preferred_element_type=f32)
    part[:, :, rank:] = back.reshape(n, samples // n, rank).astype(bf16)

    steps(far, lambda d: part_copy(d).start())
    total = part[me].astype(f32)
    if n <= 8:
        for d in near:
            part_copy(d).wait_recv()
            total = total + part_in[d].astype(f32)
    else:

        def add(i, value):
            part_copy(i + 1).wait_recv()
            return value + part_in[i + 1].astype(f32)

        total = lax.fori_loop(0, n - 1, add, total)
    reduced[...] = total.astype(bf16)
    steps(far, lambda d: full_copy(d).start())
    full[me] = reduced[...]
    steps(near, lambda d: full_copy(d).wait_recv())

    low_half = full[:, :, :rank].reshape(samples, rank)
    back_half = full[:, :, rank:].reshape(samples, rank)
    transposed = (((1,), (1,)), ((), ()))
    for f in range(features):
        cut = slice(f * width, (f + 1) * width)
        scaled = (
            lax.dot_general(low_half, up_ref[cut, :], transposed, preferred_element_type=f32)
            + bias_ref[:, cut]
        )
        wide = pooled_half[:, cut].astype(f32)
        crossed_ref[:, cut] = (wide * scaled + wide).astype(bf16)
        upstream = cot_ref[:, cut].astype(f32)
        pool_grad = (
            upstream * scaled
            + upstream
            + lax.dot_general(back_half, down_ref[cut, :], transposed, preferred_element_type=f32)
        )
        divisor = counts_ref[:, f : f + 1].astype(f32)
        grad_half[f * samples : (f + 1) * samples, :] = (pool_grad / divisor).astype(bf16)

    def send_grads(d):
        grads_out[d] = jnp.dot(place[d], grad_half[...], preferred_element_type=f32).astype(bf16)
        grads_copy(d).start()

    steps(far, send_grads)
    grads_in[0] = jnp.dot(place[0], grad_half[...], preferred_element_type=f32).astype(bf16)
    row_sum[...] = jnp.dot(owned[0], grads_in[0], preferred_element_type=f32)

    def collect(d):
        grads_copy(d).wait_recv()
        row_sum[...] += jnp.dot(owned[d], grads_in[d], preferred_element_type=f32)

    steps(near, collect)

    row_part[...] = row_sum[...].reshape(row_part.shape).astype(bf16)
    steps(group_far, lambda e: row_part_copy(e).start())
    total = row_part[group].astype(f32)
    if nr <= 8:
        for e in group_far[::-1]:
            row_part_copy(e).wait_recv()
            total = total + row_part_in[e].astype(f32)
    else:

        def add_rows(i, value):
            row_part_copy(i + 1).wait_recv()
            return value + row_part_in[i + 1].astype(f32)

        total = lax.fori_loop(0, nr - 1, add_rows, total)
    row_reduced[...] = total.astype(bf16)
    steps(group_far, lambda e: row_full_copy(e).start())
    row_full[group] = row_reduced[...]
    steps(group_far[::-1], lambda e: row_full_copy(e).wait_recv())
    grad_ref[...] = row_full[...].reshape(rows, width)

    steps(near, lambda d: rows_copy(d).wait_send())
    steps(near, lambda d: part_copy(d).wait_send())
    steps(near, lambda d: full_copy(d).wait_send())
    steps(near, lambda d: grads_copy(d).wait_send())
    steps(group_far, lambda e: row_part_copy(e).wait_send())
    steps(group_far, lambda e: row_full_copy(e).wait_send())


def shards(
    n,
    nr,
    row_table,
    grad_history,
    touched,
    lookup_slot,
    pool_counts,
    cross_down,
    cross_up,
    cross_bias,
    cotangent,
):
    rows, width = row_table.shape
    wanted = touched[0, 0]
    cap = wanted.shape[1]
    counts = pool_counts[0]
    slot_index = lookup_slot[0]
    samples, features, hot = slot_index.shape
    rank = cross_down.shape[1]
    live = jnp.arange(hot, dtype=jnp.int32)[None, None, :] < counts[:, :, None]
    slots = jnp.where(live, slot_index, -1).transpose(2, 1, 0).reshape(hot * features, samples)
    dma = pltpu.SemaphoreType.DMA
    vmem = pl.BlockSpec(memory_space=pltpu.VMEM)
    lookups = features * samples
    crossed, summed = pl.pallas_call(
        functools.partial(kernel, n, nr),
        out_shape=(
            jax.ShapeDtypeStruct((samples, features * width), bf16),
            jax.ShapeDtypeStruct((rows, width), bf16),
        ),
        in_specs=[vmem] * 8,
        out_specs=(vmem, vmem),
        scratch_shapes=[
            pltpu.VMEM((rows, width), bf16),
            pltpu.VMEM((cap, rows), bf16),
            pltpu.VMEM((n, cap, width), bf16),
            pltpu.VMEM((n, cap, width), bf16),
            pltpu.VMEM((hot * features, samples, LANES), jnp.int32),
            pltpu.VMEM((n, lookups, cap), bf16),
            pltpu.VMEM((n, cap, lookups), bf16),
            pltpu.VMEM((n, rows, cap), bf16),
            pltpu.VMEM((lookups, width), f32),
            pltpu.VMEM((samples, features * width), bf16),
            pltpu.VMEM((samples, features * width), bf16),
            pltpu.VMEM((n, samples // n, 2 * rank), bf16),
            pltpu.VMEM((n, samples // n, 2 * rank), bf16),
            pltpu.VMEM((samples // n, 2 * rank), bf16),
            pltpu.VMEM((n, samples // n, 2 * rank), bf16),
            pltpu.VMEM((lookups, width), bf16),
            pltpu.VMEM((n, cap, width), bf16),
            pltpu.VMEM((n, cap, width), bf16),
            pltpu.VMEM((rows, width), f32),
            pltpu.VMEM((nr, rows // nr, width), bf16),
            pltpu.VMEM((nr, rows // nr, width), bf16),
            pltpu.VMEM((rows // nr, width), bf16),
            pltpu.VMEM((nr, rows // nr, width), bf16),
        ]
        + [dma((n,))] * 8
        + [dma((nr,))] * 4,
        compiler_params=pltpu.CompilerParams(
            collective_id=0, has_side_effects=True, vmem_limit_bytes=56 * 1024 * 1024
        ),
        cost_estimate=pl.CostEstimate(flops=10**9 * 6, bytes_accessed=10**7, transcendentals=0),
    )(row_table, wanted, slots, counts, cross_down, cross_up, cross_bias[None, :], cotangent[0])
    summed = summed.astype(f32)
    fresh_history_sums = grad_history + summed * summed
    new_table = row_table - learn_rate * summed / (jnp.sqrt(fresh_history_sums) + epsilon)
    return (crossed[None], new_table, fresh_history_sums)


def solution(mesh):
    in_specs = (
        P("mp", None),
        P("mp", None),
        P("replica", "mp", None, None),
        P("replica", None, "mp", None),
        P("replica", None, "mp"),
        P("mp", None),
        P("mp", None),
        P("mp"),
        P("replica", None, "mp"),
    )
    out_specs = (P("replica", None, "mp"), P("mp", None), P("mp", None))
    body = functools.partial(shards, mesh.shape["mp"], mesh.shape["replica"])
    return jax.shard_map(body, mesh=mesh, in_specs=in_specs, out_specs=out_specs, check_vma=False)
```

```python
import functools

import jax
import jax.numpy as jnp
from jax import lax
from jax.experimental import pallas as pl
from jax.experimental.pallas import tpu as pltpu
from jax.sharding import PartitionSpec as P

learn_rate = 0.5
epsilon = 1e-06
LANES = 128
bf16 = jnp.bfloat16
f32 = jnp.float32


def flip(index, distance, count):
    result = 0
    bit = 1
    while bit < count:
        result = result + bit * lax.rem(
            lax.div(jnp.int32(index), jnp.int32(bit)) + lax.div(jnp.int32(distance), jnp.int32(bit)),
            jnp.int32(2),
        )
        bit *= 2
    return result


def steps(order, body):
    if len(order) <= 8:
        for d in order:
            body(d)
    else:
        first, stride = order[0], order[1] - order[0]
        lax.fori_loop(0, len(order), lambda i, c: (body(first + stride * i), c)[1], 0)


def ones_where(mask):
    return jnp.where(mask, 1.0, 0.0).astype(bf16)


def kernel(
    n,
    nr,
    table_ref,
    wanted_ref,
    slots_ref,
    counts_ref,
    down_ref,
    up_ref,
    bias_ref,
    cot_ref,
    crossed_ref,
    grad_ref,
    table_half,
    onehot,
    rows_out,
    rows_in,
    columns,
    divisors,
    pick,
    place,
    owned,
    pool_sum,
    pooled_half,
    weighted,
    mate_out,
    mate_in,
    own,
    near_out,
    far_out,
    chain_in,
    full,
    grad_half,
    grads_out,
    grads_in,
    row_sum,
    row_part,
    row_part_in,
    row_reduced,
    row_full,
    rows_send,
    rows_recv,
    grads_send,
    grads_recv,
    mate_send,
    mate_recv,
    full_send,
    full_recv,
    near_send,
    far_send,
    chain_recv,
    row_part_send,
    row_part_recv,
    row_full_send,
    row_full_recv,
):
    me = lax.axis_index("mp")
    group = lax.axis_index("replica")
    cap = wanted_ref.shape[1]
    rows, width = table_ref.shape
    features, hot, samples = slots_ref.shape
    rank = down_ref.shape[1]
    piece = min(cap, LANES)
    near = list(range(1, n))
    far = near[::-1]
    group_far = list(range(nr - 1, 0, -1))

    barrier = pltpu.get_barrier_semaphore()
    for_mp = lambda d: pl.semaphore_signal(
        barrier, inc=1, device_id={"mp": flip(me, d, n)}, device_id_type=pl.DeviceIdType.MESH
    )
    for_replica = lambda e: pl.semaphore_signal(
        barrier, inc=1, device_id={"replica": flip(group, e, nr)}, device_id_type=pl.DeviceIdType.MESH
    )
    steps(far, for_mp)
    steps(group_far, for_replica)

    def to_mp(src, dst, send, recv, d):
        return pltpu.make_async_remote_copy(
            src_ref=src,
            dst_ref=dst,
            send_sem=send.at[d],
            recv_sem=recv.at[d],
            device_id={"mp": flip(me, d, n)},
            device_id_type=pl.DeviceIdType.MESH,
        )

    def to_replica(src, dst, send, recv, e):
        return pltpu.make_async_remote_copy(
            src_ref=src,
            dst_ref=dst,
            send_sem=send.at[e],
            recv_sem=recv.at[e],
            device_id={"replica": flip(group, e, nr)},
            device_id_type=pl.DeviceIdType.MESH,
        )

    rows_copy = lambda d: to_mp(rows_out.at[d], rows_in.at[d], rows_send, rows_recv, d)
    grads_copy = lambda d: to_mp(grads_out.at[d], grads_in.at[d], grads_send, grads_recv, d)
    row_part_copy = lambda e: to_replica(
        row_part.at[flip(group, e, nr)], row_part_in.at[e], row_part_send, row_part_recv, e
    )
    row_full_copy = lambda e: to_replica(
        row_reduced, row_full.at[group], row_full_send, row_full_recv, e
    )

    pairs = n // 2
    half = lax.rem(me, jnp.int32(2))
    pair = lax.div(me, jnp.int32(2))
    upper = lax.div(2 * pair, jnp.int32(pairs))
    depth = pair + upper * (pairs - 1 - 2 * pair)
    middle = lax.div(depth + 1, jnp.int32(pairs // 2))
    mate = me + 1 - 2 * half
    inward = me + 2 * (1 - 2 * upper)
    outward = me - 2 * (1 - 2 * upper)
    chunks = mate_out.shape[0]

    def to_device(src, dst, send, recv, device):
        return pltpu.make_async_remote_copy(
            src_ref=src,
            dst_ref=dst,
            send_sem=send,
            recv_sem=recv,
            device_id={"mp": device},
            device_id_type=pl.DeviceIdType.MESH,
        )

    mate_copy = lambda c: to_device(
        mate_out.at[c], mate_in.at[c], mate_send.at[c], mate_recv.at[c], mate
    )
    full_copy = lambda h, c: to_device(
        full.at[h, c], full.at[h, c], full_send.at[c], full_recv.at[c], mate
    )
    near_copy = lambda slot, c: to_device(
        near_out.at[c], chain_in.at[slot, c], near_send.at[c], chain_recv.at[slot, c], inward
    )
    far_copy = lambda c: to_device(
        far_out.at[c], chain_in.at[1, c], far_send.at[c], chain_recv.at[1, c], outward
    )

    table_half[...] = table_ref[...].astype(bf16)
    lane = lax.broadcasted_iota(jnp.int32, (cap, LANES), 1)

    def gather(d):
        row = wanted_ref[pl.ds(flip(me, d, n), 1), :]
        column = jnp.broadcast_to(row, (LANES, cap)).T
        for j in range(rows // LANES):
            onehot[:, j * LANES : (j + 1) * LANES] = ones_where(column == lane + j * LANES)
        return jnp.dot(onehot[...], table_half[...], preferred_element_type=f32).astype(bf16)

    rows_out[n - 1] = gather(n - 1)
    pl.semaphore_wait(barrier, n - 1 + nr - 1)
    rows_copy(n - 1).start()

    def send_rows(d):
        rows_out[d] = gather(d)
        rows_copy(d).start()

    steps(far[1:], send_rows)
    rows_in[0] = gather(0)

    slot_rows = {}
    for f in range(features):
        count = counts_ref[f : f + 1, :]
        divisors[f] = jnp.broadcast_to(count.astype(f32), (width, samples)).T
        for k in range(hot):
            row = jnp.where(k < count, slots_ref[f, k : k + 1, :], -1)
            slot_rows[f, k] = row
            columns[k * features + f] = jnp.broadcast_to(row, (LANES, samples)).T
    piece_lane = lax.broadcasted_iota(jnp.int32, (samples, piece), 1)
    cap_row = lax.broadcasted_iota(jnp.int32, (cap, samples), 0)
    block_row = lax.broadcasted_iota(jnp.int32, (LANES, cap), 0)

    def build_pick(d):
        base = flip(me, d, n) * cap
        for f in range(features):
            for j in range(cap // piece):
                mask = None
                for k in range(hot):
                    hit = columns[k * features + f][:, :piece] - (base + j * piece) == piece_lane
                    mask = hit if mask is None else mask | hit
                pick[d, f * samples : (f + 1) * samples, j * piece : (j + 1) * piece] = ones_where(mask)

    def build_place(d):
        base = flip(me, d, n) * cap
        for f in range(features):
            mask = None
            for k in range(hot):
                hit = slot_rows[f, k] - base == cap_row
                mask = hit if mask is None else mask | hit
            place[d, :, f * samples : (f + 1) * samples] = ones_where(mask)

    def build_owned(d):
        row = wanted_ref[pl.ds(flip(me, d, n), 1), :]
        for j in range(rows // LANES):
            owned[d, j * LANES : (j + 1) * LANES, :] = ones_where(row == block_row + j * LANES)

    steps([0] + near, build_pick)
    pool_sum[...] = jnp.dot(pick[0], rows_in[0], preferred_element_type=f32)
    steps([0] + near, build_place)
    steps([0] + near, build_owned)

    def pool(d):
        rows_copy(d).wait_recv()
        pool_sum[...] += jnp.dot(pick[d], rows_in[d], preferred_element_type=f32)

    steps(near, pool)

    rows_half = samples // 2
    for f in range(features):
        cut = slice(f * width, (f + 1) * width)
        value = (pool_sum[f * samples : (f + 1) * samples, :] / divisors[f]).astype(bf16)
        change = (cot_ref[:, cut].astype(f32) * value.astype(f32)).astype(bf16)
        for h in range(2):
            pooled_half[h, :, cut] = value[h * rows_half : (h + 1) * rows_half]
            weighted[h, :, cut] = change[h * rows_half : (h + 1) * rows_half]

    def partial(h):
        low = jnp.dot(pooled_half[h], down_ref[...], preferred_element_type=f32)
        back = jnp.dot(weighted[h], up_ref[...], preferred_element_type=f32)
        return low.reshape(chunks, -1, rank), back.reshape(chunks, -1, rank)

    low, back = partial(1 - half)
    mate_out[:, :, :rank] = low.astype(bf16)
    mate_out[:, :, rank:] = back.astype(bf16)
    for c in range(chunks):
        mate_copy(c).start()
    low, back = partial(half)
    own[:, :, :rank] = low
    own[:, :, rank:] = back

    def near_step(c):
        mate_copy(c).wait_recv()
        own[c] = own[c] + mate_in[c].astype(f32)

        @pl.when(depth == 0)
        def _():
            near_out[c] = own[c].astype(bf16)

        @pl.when(depth > 0)
        def _():
            near_copy(0, c).wait_recv()
            near_out[c] = (own[c] + chain_in[0, c].astype(f32)).astype(bf16)

        near_copy(middle, c).start()

    def far_step(c):
        near_copy(1, c).wait_recv()
        value = own[c] + chain_in[1, c].astype(f32)

        @pl.when(depth == 0)
        def _():
            full[half, c] = value.astype(bf16)

        @pl.when(depth > 0)
        def _():
            far_out[c] = value.astype(bf16)
            far_copy(c).start()
            full[half, c] = (value + chain_in[0, c].astype(f32)).astype(bf16)

        full_copy(half, c).start()

    lag = 3
    for t in range(chunks + lag):
        if t < chunks:
            near_step(t)
        if t >= lag:
            far_step(t - lag)
    for c in range(chunks):
        full_copy(1 - half, c).wait_recv()

    low_half = full[:, :, :, :rank].reshape(samples, rank)
    back_half = full[:, :, :, rank:].reshape(samples, rank)
    transposed = (((1,), (1,)), ((), ()))
    for f in range(features):
        cut = slice(f * width, (f + 1) * width)
        scaled = (
            lax.dot_general(low_half, up_ref[cut, :], transposed, preferred_element_type=f32)
            + bias_ref[:, cut]
        )
        wide = pooled_half[:, :, cut].reshape(samples, width).astype(f32)
        crossed_ref[:, cut] = (wide * scaled + wide).astype(bf16)
        upstream = cot_ref[:, cut].astype(f32)
        pool_grad = (
            upstream * scaled
            + upstream
            + lax.dot_general(back_half, down_ref[cut, :], transposed, preferred_element_type=f32)
        )
        grad_half[f * samples : (f + 1) * samples, :] = (pool_grad / divisors[f]).astype(bf16)

    def send_grads(d):
        grads_out[d] = jnp.dot(place[d], grad_half[...], preferred_element_type=f32).astype(bf16)
        grads_copy(d).start()

    steps(far, send_grads)
    grads_in[0] = jnp.dot(place[0], grad_half[...], preferred_element_type=f32).astype(bf16)
    row_sum[...] = jnp.dot(owned[0], grads_in[0], preferred_element_type=f32)

    def collect(d):
        grads_copy(d).wait_recv()
        row_sum[...] += jnp.dot(owned[d], grads_in[d], preferred_element_type=f32)

    steps(near, collect)

    row_part[...] = row_sum[...].reshape(row_part.shape).astype(bf16)
    steps(group_far, lambda e: row_part_copy(e).start())
    total = row_part[group].astype(f32)
    if nr <= 8:
        for e in group_far[::-1]:
            row_part_copy(e).wait_recv()
            total = total + row_part_in[e].astype(f32)
    else:

        def add_rows(i, value):
            row_part_copy(i + 1).wait_recv()
            return value + row_part_in[i + 1].astype(f32)

        total = lax.fori_loop(0, nr - 1, add_rows, total)
    row_reduced[...] = total.astype(bf16)
    steps(group_far, lambda e: row_full_copy(e).start())
    row_full[group] = row_reduced[...]
    steps(group_far[::-1], lambda e: row_full_copy(e).wait_recv())
    grad_ref[...] = row_full[...].reshape(rows, width)

    steps(near, lambda d: rows_copy(d).wait_send())
    for c in range(chunks):
        mate_copy(c).wait_send()
        near_copy(middle, c).wait_send()
        full_copy(half, c).wait_send()

    @pl.when(depth > 0)
    def _():
        for c in range(chunks):
            far_copy(c).wait_send()

    steps(near, lambda d: grads_copy(d).wait_send())
    steps(group_far, lambda e: row_part_copy(e).wait_send())
    steps(group_far, lambda e: row_full_copy(e).wait_send())


def shards(
    n,
    nr,
    row_table,
    grad_history,
    touched,
    lookup_slot,
    pool_counts,
    cross_down,
    cross_up,
    cross_bias,
    cotangent,
):
    rows, width = row_table.shape
    wanted = touched[0, 0]
    cap = wanted.shape[1]
    counts = pool_counts[0].T
    slots = lookup_slot[0].transpose(1, 2, 0)
    features, hot, samples = slots.shape
    rank = cross_down.shape[1]
    dma = pltpu.SemaphoreType.DMA
    vmem = pl.BlockSpec(memory_space=pltpu.VMEM)
    lookups = features * samples
    chunks = samples // 32
    chunk = (chunks, 16, 2 * rank)
    crossed, summed = pl.pallas_call(
        functools.partial(kernel, n, nr),
        out_shape=(
            jax.ShapeDtypeStruct((samples, features * width), bf16),
            jax.ShapeDtypeStruct((rows, width), bf16),
        ),
        in_specs=[vmem] * 8,
        out_specs=(vmem, vmem),
        scratch_shapes=[
            pltpu.VMEM((rows, width), bf16),
            pltpu.VMEM((cap, rows), bf16),
            pltpu.VMEM((n, cap, width), bf16),
            pltpu.VMEM((n, cap, width), bf16),
            pltpu.VMEM((hot * features, samples, LANES), jnp.int32),
            pltpu.VMEM((features, samples, width), f32),
            pltpu.VMEM((n, lookups, cap), bf16),
            pltpu.VMEM((n, cap, lookups), bf16),
            pltpu.VMEM((n, rows, cap), bf16),
            pltpu.VMEM((lookups, width), f32),
            pltpu.VMEM((2, samples // 2, features * width), bf16),
            pltpu.VMEM((2, samples // 2, features * width), bf16),
            pltpu.VMEM(chunk, bf16),
            pltpu.VMEM(chunk, bf16),
            pltpu.VMEM(chunk, f32),
            pltpu.VMEM(chunk, bf16),
            pltpu.VMEM(chunk, bf16),
            pltpu.VMEM((2, *chunk), bf16),
            pltpu.VMEM((2, *chunk), bf16),
            pltpu.VMEM((lookups, width), bf16),
            pltpu.VMEM((n, cap, width), bf16),
            pltpu.VMEM((n, cap, width), bf16),
            pltpu.VMEM((rows, width), f32),
            pltpu.VMEM((nr, rows // nr, width), bf16),
            pltpu.VMEM((nr, rows // nr, width), bf16),
            pltpu.VMEM((rows // nr, width), bf16),
            pltpu.VMEM((nr, rows // nr, width), bf16),
        ]
        + [dma((n,))] * 4
        + [dma((chunks,))] * 6
        + [dma((2, chunks))]
        + [dma((nr,))] * 4,
        compiler_params=pltpu.CompilerParams(
            collective_id=0, has_side_effects=True, vmem_limit_bytes=56 * 1024 * 1024
        ),
        cost_estimate=pl.CostEstimate(flops=10**9 * 6, bytes_accessed=10**7, transcendentals=0),
    )(row_table, wanted, slots, counts, cross_down, cross_up, cross_bias[None, :], cotangent[0])
    summed = summed.astype(f32)
    fresh_history_sums = grad_history + summed * summed
    new_table = row_table - learn_rate * summed / (jnp.sqrt(fresh_history_sums) + epsilon)
    return (crossed[None], new_table, fresh_history_sums)


def solution(mesh):
    in_specs = (
        P("mp", None),
        P("mp", None),
        P("replica", "mp", None, None),
        P("replica", None, "mp", None),
        P("replica", None, "mp"),
        P("mp", None),
        P("mp", None),
        P("mp"),
        P("replica", None, "mp"),
    )
    out_specs = (P("replica", None, "mp"), P("mp", None), P("mp", None))
    body = functools.partial(shards, mesh.shape["mp"], mesh.shape["replica"])
    return jax.shard_map(body, mesh=mesh, in_specs=in_specs, out_specs=out_specs, check_vma=False)
```

```python
import functools

import jax
import jax.numpy as jnp
from jax import lax
from jax.experimental import pallas as pl
from jax.experimental.pallas import tpu as pltpu
from jax.sharding import PartitionSpec as P

learn_rate = 0.5
epsilon = 1e-06
LANES = 128
bf16 = jnp.bfloat16
f32 = jnp.float32


def flip(index, distance, count):
    result = 0
    bit = 1
    while bit < count:
        result = result + bit * lax.rem(
            lax.div(jnp.int32(index), jnp.int32(bit)) + lax.div(jnp.int32(distance), jnp.int32(bit)),
            jnp.int32(2),
        )
        bit *= 2
    return result


def steps(order, body):
    if len(order) <= 8:
        for d in order:
            body(d)
    else:
        first, stride = order[0], order[1] - order[0]
        lax.fori_loop(0, len(order), lambda i, c: (body(first + stride * i), c)[1], 0)


def ones_where(mask):
    return jnp.where(mask, 1.0, 0.0).astype(bf16)


def kernel(
    n,
    nr,
    table_ref,
    wanted_ref,
    slots_ref,
    counts_ref,
    down_ref,
    up_ref,
    bias_ref,
    cot_ref,
    crossed_ref,
    grad_ref,
    table_half,
    onehot,
    rows_out,
    rows_in,
    columns,
    divisors,
    pick,
    place,
    owned,
    pool_sum,
    pooled_half,
    weighted,
    mate_out,
    mate_in,
    own,
    pair_out,
    pair_in,
    full,
    grad_half,
    grads_out,
    grads_in,
    row_sum,
    row_part,
    row_part_in,
    row_reduced,
    row_full,
    rows_send,
    rows_recv,
    grads_send,
    grads_recv,
    mate_send,
    mate_recv,
    pair_send,
    pair_recv,
    full_send,
    full_recv,
    pass_send,
    pass_recv,
    row_part_send,
    row_part_recv,
    row_full_send,
    row_full_recv,
):
    me = lax.axis_index("mp")
    group = lax.axis_index("replica")
    cap = wanted_ref.shape[1]
    rows, width = table_ref.shape
    features, hot, samples = slots_ref.shape
    rank = down_ref.shape[1]
    piece = min(cap, LANES)
    near = list(range(1, n))
    far = near[::-1]
    group_far = list(range(nr - 1, 0, -1))

    barrier = pltpu.get_barrier_semaphore()
    for_mp = lambda d: pl.semaphore_signal(
        barrier, inc=1, device_id={"mp": flip(me, d, n)}, device_id_type=pl.DeviceIdType.MESH
    )
    for_replica = lambda e: pl.semaphore_signal(
        barrier, inc=1, device_id={"replica": flip(group, e, nr)}, device_id_type=pl.DeviceIdType.MESH
    )
    steps(far, for_mp)
    steps(group_far, for_replica)

    def to_mp(src, dst, send, recv, d):
        return pltpu.make_async_remote_copy(
            src_ref=src,
            dst_ref=dst,
            send_sem=send.at[d],
            recv_sem=recv.at[d],
            device_id={"mp": flip(me, d, n)},
            device_id_type=pl.DeviceIdType.MESH,
        )

    def to_replica(src, dst, send, recv, e):
        return pltpu.make_async_remote_copy(
            src_ref=src,
            dst_ref=dst,
            send_sem=send.at[e],
            recv_sem=recv.at[e],
            device_id={"replica": flip(group, e, nr)},
            device_id_type=pl.DeviceIdType.MESH,
        )

    rows_copy = lambda d: to_mp(rows_out.at[d], rows_in.at[d], rows_send, rows_recv, d)
    grads_copy = lambda d: to_mp(grads_out.at[d], grads_in.at[d], grads_send, grads_recv, d)
    row_part_copy = lambda e: to_replica(
        row_part.at[flip(group, e, nr)], row_part_in.at[e], row_part_send, row_part_recv, e
    )
    row_full_copy = lambda e: to_replica(
        row_reduced, row_full.at[group], row_full_send, row_full_recv, e
    )

    pairs = n // 2
    half = lax.rem(me, jnp.int32(2))
    pair = lax.div(me, jnp.int32(2))
    mate = me + 1 - 2 * half
    pair_near = list(range(1, pairs))
    pair_far = pair_near[::-1]

    def to_device(src, dst, send, recv, device):
        return pltpu.make_async_remote_copy(
            src_ref=src,
            dst_ref=dst,
            send_sem=send,
            recv_sem=recv,
            device_id={"mp": device},
            device_id_type=pl.DeviceIdType.MESH,
        )

    across = lambda e: flip(pair, e, pairs)
    mate_copy = lambda e: to_device(
        mate_out.at[across(e)], mate_in.at[e], mate_send.at[e], mate_recv.at[e], mate
    )
    pair_copy = lambda e: to_device(
        pair_out.at[e], pair_in.at[e], pair_send.at[e], pair_recv.at[e], 2 * across(e) + half
    )
    full_copy = lambda e: to_device(
        full.at[half, pair],
        full.at[half, pair],
        full_send.at[e],
        full_recv.at[e],
        2 * across(e) + half,
    )
    pass_copy = lambda h, e: to_device(
        full.at[h, across(e)], full.at[h, across(e)], pass_send.at[e], pass_recv.at[e], mate
    )

    table_half[...] = table_ref[...].astype(bf16)
    lane = lax.broadcasted_iota(jnp.int32, (cap, LANES), 1)

    def gather(d):
        row = wanted_ref[pl.ds(flip(me, d, n), 1), :]
        column = jnp.broadcast_to(row, (LANES, cap)).T
        for j in range(rows // LANES):
            onehot[:, j * LANES : (j + 1) * LANES] = ones_where(column == lane + j * LANES)
        return jnp.dot(onehot[...], table_half[...], preferred_element_type=f32).astype(bf16)

    rows_out[n - 1] = gather(n - 1)
    pl.semaphore_wait(barrier, n - 1 + nr - 1)
    rows_copy(n - 1).start()

    def send_rows(d):
        rows_out[d] = gather(d)
        rows_copy(d).start()

    steps(far[1:], send_rows)
    rows_in[0] = gather(0)

    slot_rows = {}
    for f in range(features):
        count = counts_ref[f : f + 1, :]
        divisors[f] = jnp.broadcast_to(count.astype(f32), (width, samples)).T
        for k in range(hot):
            row = jnp.where(k < count, slots_ref[f, k : k + 1, :], -1)
            slot_rows[f, k] = row
            columns[k * features + f] = jnp.broadcast_to(row, (LANES, samples)).T
    piece_lane = lax.broadcasted_iota(jnp.int32, (samples, piece), 1)
    cap_row = lax.broadcasted_iota(jnp.int32, (cap, samples), 0)
    block_row = lax.broadcasted_iota(jnp.int32, (LANES, cap), 0)

    def build_pick(d):
        base = flip(me, d, n) * cap
        for f in range(features):
            for j in range(cap // piece):
                mask = None
                for k in range(hot):
                    hit = columns[k * features + f][:, :piece] - (base + j * piece) == piece_lane
                    mask = hit if mask is None else mask | hit
                pick[d, f * samples : (f + 1) * samples, j * piece : (j + 1) * piece] = ones_where(mask)

    def build_place(d):
        base = flip(me, d, n) * cap
        for f in range(features):
            mask = None
            for k in range(hot):
                hit = slot_rows[f, k] - base == cap_row
                mask = hit if mask is None else mask | hit
            place[d, :, f * samples : (f + 1) * samples] = ones_where(mask)

    def build_owned(d):
        row = wanted_ref[pl.ds(flip(me, d, n), 1), :]
        for j in range(rows // LANES):
            owned[d, j * LANES : (j + 1) * LANES, :] = ones_where(row == block_row + j * LANES)

    steps([0] + near, build_pick)
    pool_sum[...] = jnp.dot(pick[0], rows_in[0], preferred_element_type=f32)
    steps([0] + near, build_place)
    steps([0] + near, build_owned)

    def pool(d):
        rows_copy(d).wait_recv()
        pool_sum[...] += jnp.dot(pick[d], rows_in[d], preferred_element_type=f32)

    steps(near, pool)

    rows_half = samples // 2
    for f in range(features):
        cut = slice(f * width, (f + 1) * width)
        value = (pool_sum[f * samples : (f + 1) * samples, :] / divisors[f]).astype(bf16)
        change = (cot_ref[:, cut].astype(f32) * value.astype(f32)).astype(bf16)
        for h in range(2):
            pooled_half[h, :, cut] = value[h * rows_half : (h + 1) * rows_half]
            weighted[h, :, cut] = change[h * rows_half : (h + 1) * rows_half]

    def partial(h):
        low = jnp.dot(pooled_half[h], down_ref[...], preferred_element_type=f32)
        back = jnp.dot(weighted[h], up_ref[...], preferred_element_type=f32)
        return low.reshape(pairs, -1, rank), back.reshape(pairs, -1, rank)

    low, back = partial(1 - half)
    mate_out[:, :, :rank] = low.astype(bf16)
    mate_out[:, :, rank:] = back.astype(bf16)
    steps(pair_far + [0], lambda e: mate_copy(e).start())
    low, back = partial(half)
    own[:, :, :rank] = low
    own[:, :, rank:] = back

    def send_pair(e):
        mate_copy(e).wait_recv()
        pair_out[e] = (own[across(e)] + mate_in[e].astype(f32)).astype(bf16)
        pair_copy(e).start()

    steps(pair_far, send_pair)
    mate_copy(0).wait_recv()
    own[pair] = own[pair] + mate_in[0].astype(f32)

    def add_pair(e):
        pair_copy(e).wait_recv()
        own[pair] = own[pair] + pair_in[e].astype(f32)

    steps(pair_near, add_pair)
    full[half, pair] = own[pair].astype(bf16)
    steps(pair_far, lambda e: full_copy(e).start())
    pass_copy(half, 0).start()

    def pass_on(e):
        full_copy(e).wait_recv()
        pass_copy(half, e).start()

    steps(pair_near, pass_on)
    steps([0] + pair_near, lambda e: pass_copy(1 - half, e).wait_recv())

    low_half = full[:, :, :, :rank].reshape(samples, rank)
    back_half = full[:, :, :, rank:].reshape(samples, rank)
    transposed = (((1,), (1,)), ((), ()))
    for f in range(features):
        cut = slice(f * width, (f + 1) * width)
        scaled = (
            lax.dot_general(low_half, up_ref[cut, :], transposed, preferred_element_type=f32)
            + bias_ref[:, cut]
        )
        wide = pooled_half[:, :, cut].reshape(samples, width).astype(f32)
        crossed_ref[:, cut] = (wide * scaled + wide).astype(bf16)
        upstream = cot_ref[:, cut].astype(f32)
        pool_grad = (
            upstream * scaled
            + upstream
            + lax.dot_general(back_half, down_ref[cut, :], transposed, preferred_element_type=f32)
        )
        grad_half[f * samples : (f + 1) * samples, :] = (pool_grad / divisors[f]).astype(bf16)

    def send_grads(d):
        grads_out[d] = jnp.dot(place[d], grad_half[...], preferred_element_type=f32).astype(bf16)
        grads_copy(d).start()

    steps(far, send_grads)
    grads_in[0] = jnp.dot(place[0], grad_half[...], preferred_element_type=f32).astype(bf16)
    row_sum[...] = jnp.dot(owned[0], grads_in[0], preferred_element_type=f32)

    def collect(d):
        grads_copy(d).wait_recv()
        row_sum[...] += jnp.dot(owned[d], grads_in[d], preferred_element_type=f32)

    steps(near, collect)

    row_part[...] = row_sum[...].reshape(row_part.shape).astype(bf16)
    steps(group_far, lambda e: row_part_copy(e).start())
    total = row_part[group].astype(f32)
    if nr <= 8:
        for e in group_far[::-1]:
            row_part_copy(e).wait_recv()
            total = total + row_part_in[e].astype(f32)
    else:

        def add_rows(i, value):
            row_part_copy(i + 1).wait_recv()
            return value + row_part_in[i + 1].astype(f32)

        total = lax.fori_loop(0, nr - 1, add_rows, total)
    row_reduced[...] = total.astype(bf16)
    steps(group_far, lambda e: row_full_copy(e).start())
    row_full[group] = row_reduced[...]
    steps(group_far[::-1], lambda e: row_full_copy(e).wait_recv())
    grad_ref[...] = row_full[...].reshape(rows, width)

    steps(near, lambda d: rows_copy(d).wait_send())
    steps([0] + pair_near, lambda e: mate_copy(e).wait_send())
    steps(pair_near, lambda e: pair_copy(e).wait_send())
    steps(pair_near, lambda e: full_copy(e).wait_send())
    steps([0] + pair_near, lambda e: pass_copy(half, e).wait_send())
    steps(near, lambda d: grads_copy(d).wait_send())
    steps(group_far, lambda e: row_part_copy(e).wait_send())
    steps(group_far, lambda e: row_full_copy(e).wait_send())


def shards(
    n,
    nr,
    row_table,
    grad_history,
    touched,
    lookup_slot,
    pool_counts,
    cross_down,
    cross_up,
    cross_bias,
    cotangent,
):
    rows, width = row_table.shape
    wanted = touched[0, 0]
    cap = wanted.shape[1]
    counts = pool_counts[0].T
    slots = lookup_slot[0].transpose(1, 2, 0)
    features, hot, samples = slots.shape
    rank = cross_down.shape[1]
    dma = pltpu.SemaphoreType.DMA
    vmem = pl.BlockSpec(memory_space=pltpu.VMEM)
    lookups = features * samples
    pieces = (n // 2, samples // n, 2 * rank)
    crossed, summed = pl.pallas_call(
        functools.partial(kernel, n, nr),
        out_shape=(
            jax.ShapeDtypeStruct((samples, features * width), bf16),
            jax.ShapeDtypeStruct((rows, width), bf16),
        ),
        in_specs=[vmem] * 8,
        out_specs=(vmem, vmem),
        scratch_shapes=[
            pltpu.VMEM((rows, width), bf16),
            pltpu.VMEM((cap, rows), bf16),
            pltpu.VMEM((n, cap, width), bf16),
            pltpu.VMEM((n, cap, width), bf16),
            pltpu.VMEM((hot * features, samples, LANES), jnp.int32),
            pltpu.VMEM((features, samples, width), f32),
            pltpu.VMEM((n, lookups, cap), bf16),
            pltpu.VMEM((n, cap, lookups), bf16),
            pltpu.VMEM((n, rows, cap), bf16),
            pltpu.VMEM((lookups, width), f32),
            pltpu.VMEM((2, samples // 2, features * width), bf16),
            pltpu.VMEM((2, samples // 2, features * width), bf16),
            pltpu.VMEM(pieces, bf16),
            pltpu.VMEM(pieces, bf16),
            pltpu.VMEM(pieces, f32),
            pltpu.VMEM(pieces, bf16),
            pltpu.VMEM(pieces, bf16),
            pltpu.VMEM((2, *pieces), bf16),
            pltpu.VMEM((lookups, width), bf16),
            pltpu.VMEM((n, cap, width), bf16),
            pltpu.VMEM((n, cap, width), bf16),
            pltpu.VMEM((rows, width), f32),
            pltpu.VMEM((nr, rows // nr, width), bf16),
            pltpu.VMEM((nr, rows // nr, width), bf16),
            pltpu.VMEM((rows // nr, width), bf16),
            pltpu.VMEM((nr, rows // nr, width), bf16),
        ]
        + [dma((n,))] * 4
        + [dma((n // 2,))] * 8
        + [dma((nr,))] * 4,
        compiler_params=pltpu.CompilerParams(
            collective_id=0, has_side_effects=True, vmem_limit_bytes=56 * 1024 * 1024
        ),
        cost_estimate=pl.CostEstimate(flops=10**9 * 6, bytes_accessed=10**7, transcendentals=0),
    )(row_table, wanted, slots, counts, cross_down, cross_up, cross_bias[None, :], cotangent[0])
    summed = summed.astype(f32)
    fresh_history_sums = grad_history + summed * summed
    new_table = row_table - learn_rate * summed / (jnp.sqrt(fresh_history_sums) + epsilon)
    return (crossed[None], new_table, fresh_history_sums)


def solution(mesh):
    in_specs = (
        P("mp", None),
        P("mp", None),
        P("replica", "mp", None, None),
        P("replica", None, "mp", None),
        P("replica", None, "mp"),
        P("mp", None),
        P("mp", None),
        P("mp"),
        P("replica", None, "mp"),
    )
    out_specs = (P("replica", None, "mp"), P("mp", None), P("mp", None))
    body = functools.partial(shards, mesh.shape["mp"], mesh.shape["replica"])
    return jax.shard_map(body, mesh=mesh, in_specs=in_specs, out_specs=out_specs, check_vma=False)
```

```python
import functools

import jax
import jax.numpy as jnp
from jax import lax
from jax.experimental import pallas as pl
from jax.experimental.pallas import tpu as pltpu
from jax.sharding import PartitionSpec as P

learn_rate = 0.5
epsilon = 1e-06
LANES = 128
bf16 = jnp.bfloat16
f32 = jnp.float32


def flip(index, distance, count):
    result = 0
    bit = 1
    while bit < count:
        result = result + bit * lax.rem(
            lax.div(jnp.int32(index), jnp.int32(bit)) + lax.div(jnp.int32(distance), jnp.int32(bit)),
            jnp.int32(2),
        )
        bit *= 2
    return result


def steps(order, body):
    if len(order) <= 8:
        for d in order:
            body(d)
    else:
        first, stride = order[0], order[1] - order[0]
        lax.fori_loop(0, len(order), lambda i, c: (body(first + stride * i), c)[1], 0)


def ones_where(mask):
    return jnp.where(mask, 1.0, 0.0).astype(bf16)


def kernel(
    n,
    nr,
    table_ref,
    wanted_ref,
    slots_ref,
    counts_ref,
    down_ref,
    up_ref,
    bias_ref,
    cot_ref,
    crossed_ref,
    grad_ref,
    table_half,
    onehot,
    rows_out,
    rows_in,
    columns,
    divisors,
    pick,
    place,
    owned,
    pool_sum,
    pooled_half,
    weighted,
    mate_out,
    mate_in,
    own,
    pair_out,
    pair_in,
    full,
    grad_half,
    grads_out,
    grads_in,
    row_sum,
    row_part,
    row_part_in,
    row_total,
    row_full,
    rows_send,
    rows_recv,
    grads_send,
    grads_recv,
    mate_send,
    mate_recv,
    pair_send,
    pair_recv,
    full_send,
    full_recv,
    pass_send,
    pass_recv,
    row_part_send,
    row_part_recv,
    row_full_send,
    row_full_recv,
):
    me = lax.axis_index("mp")
    group = lax.axis_index("replica")
    cap = wanted_ref.shape[1]
    rows, width = table_ref.shape
    features, hot, samples = slots_ref.shape
    rank = down_ref.shape[1]
    piece = min(cap, LANES)
    near = list(range(1, n))
    far = near[::-1]
    group_far = list(range(nr - 1, 0, -1))

    barrier = pltpu.get_barrier_semaphore()
    for_mp = lambda d: pl.semaphore_signal(
        barrier, inc=1, device_id={"mp": flip(me, d, n)}, device_id_type=pl.DeviceIdType.MESH
    )
    for_replica = lambda e: pl.semaphore_signal(
        barrier, inc=1, device_id={"replica": flip(group, e, nr)}, device_id_type=pl.DeviceIdType.MESH
    )
    steps(far, for_mp)
    steps(group_far, for_replica)

    def to_mp(src, dst, send, recv, d):
        return pltpu.make_async_remote_copy(
            src_ref=src,
            dst_ref=dst,
            send_sem=send.at[d],
            recv_sem=recv.at[d],
            device_id={"mp": flip(me, d, n)},
            device_id_type=pl.DeviceIdType.MESH,
        )

    def to_replica(src, dst, send, recv, e):
        return pltpu.make_async_remote_copy(
            src_ref=src,
            dst_ref=dst,
            send_sem=send.at[e],
            recv_sem=recv.at[e],
            device_id={"replica": flip(group, e, nr)},
            device_id_type=pl.DeviceIdType.MESH,
        )

    rows_copy = lambda d: to_mp(rows_out.at[d], rows_in.at[d], rows_send, rows_recv, d)
    grads_copy = lambda h, d: to_mp(
        grads_out.at[h, d], grads_in.at[h, d], grads_send.at[h], grads_recv.at[h], d
    )
    row_part_copy = lambda h, e: to_replica(
        row_part.at[h, flip(group, e, nr)],
        row_part_in.at[h, e],
        row_part_send.at[h],
        row_part_recv.at[h],
        e,
    )
    row_full_copy = lambda h, e: to_replica(
        row_full.at[h, group], row_full.at[h, group], row_full_send.at[h], row_full_recv.at[h], e
    )

    pairs = n // 2
    half = lax.rem(me, jnp.int32(2))
    pair = lax.div(me, jnp.int32(2))
    mate = me + 1 - 2 * half
    pair_near = list(range(1, pairs))
    pair_far = pair_near[::-1]

    def to_device(src, dst, send, recv, device):
        return pltpu.make_async_remote_copy(
            src_ref=src,
            dst_ref=dst,
            send_sem=send,
            recv_sem=recv,
            device_id={"mp": device},
            device_id_type=pl.DeviceIdType.MESH,
        )

    across = lambda e: flip(pair, e, pairs)
    mate_copy = lambda e: to_device(
        mate_out.at[across(e)], mate_in.at[e], mate_send.at[e], mate_recv.at[e], mate
    )
    pair_copy = lambda e: to_device(
        pair_out.at[e], pair_in.at[e], pair_send.at[e], pair_recv.at[e], 2 * across(e) + half
    )
    full_copy = lambda e: to_device(
        full.at[half, pair],
        full.at[half, pair],
        full_send.at[e],
        full_recv.at[e],
        2 * across(e) + half,
    )
    pass_copy = lambda h, e: to_device(
        full.at[h, across(e)], full.at[h, across(e)], pass_send.at[e], pass_recv.at[e], mate
    )

    table_half[...] = table_ref[...].astype(bf16)
    lane = lax.broadcasted_iota(jnp.int32, (cap, LANES), 1)

    def gather(d):
        row = wanted_ref[pl.ds(flip(me, d, n), 1), :]
        column = jnp.broadcast_to(row, (LANES, cap)).T
        for j in range(rows // LANES):
            onehot[:, j * LANES : (j + 1) * LANES] = ones_where(column == lane + j * LANES)
        return jnp.dot(onehot[...], table_half[...], preferred_element_type=f32).astype(bf16)

    rows_out[n - 1] = gather(n - 1)
    pl.semaphore_wait(barrier, n - 1 + nr - 1)
    rows_copy(n - 1).start()

    def send_rows(d):
        rows_out[d] = gather(d)
        rows_copy(d).start()

    steps(far[1:], send_rows)
    rows_in[0] = gather(0)

    slot_rows = {}
    for f in range(features):
        count = counts_ref[f : f + 1, :]
        divisors[f] = jnp.broadcast_to(count.astype(f32), (width, samples)).T
        for k in range(hot):
            row = jnp.where(k < count, slots_ref[f, k : k + 1, :], -1)
            slot_rows[f, k] = row
            columns[k * features + f] = jnp.broadcast_to(row, (LANES, samples)).T
    piece_lane = lax.broadcasted_iota(jnp.int32, (samples, piece), 1)
    cap_row = lax.broadcasted_iota(jnp.int32, (cap, samples), 0)
    block_row = lax.broadcasted_iota(jnp.int32, (LANES, cap), 0)

    def build_pick(d):
        base = flip(me, d, n) * cap
        for f in range(features):
            for j in range(cap // piece):
                mask = None
                for k in range(hot):
                    hit = columns[k * features + f][:, :piece] - (base + j * piece) == piece_lane
                    mask = hit if mask is None else mask | hit
                pick[d, f * samples : (f + 1) * samples, j * piece : (j + 1) * piece] = ones_where(mask)

    def build_place(d):
        base = flip(me, d, n) * cap
        for f in range(features):
            mask = None
            for k in range(hot):
                hit = slot_rows[f, k] - base == cap_row
                mask = hit if mask is None else mask | hit
            place[d, :, f * samples : (f + 1) * samples] = ones_where(mask)

    def build_owned(d):
        row = wanted_ref[pl.ds(flip(me, d, n), 1), :]
        for j in range(rows // LANES):
            owned[d, j * LANES : (j + 1) * LANES, :] = ones_where(row == block_row + j * LANES)

    steps([0] + near, build_pick)
    pool_sum[...] = jnp.dot(pick[0], rows_in[0], preferred_element_type=f32)

    def pool(d):
        rows_copy(d).wait_recv()
        pool_sum[...] += jnp.dot(pick[d], rows_in[d], preferred_element_type=f32)

    steps(near, pool)

    rows_half = samples // 2
    for f in range(features):
        cut = slice(f * width, (f + 1) * width)
        value = (pool_sum[f * samples : (f + 1) * samples, :] / divisors[f]).astype(bf16)
        change = (cot_ref[:, cut].astype(f32) * value.astype(f32)).astype(bf16)
        for h in range(2):
            pooled_half[h, :, cut] = value[h * rows_half : (h + 1) * rows_half]
            weighted[h, :, cut] = change[h * rows_half : (h + 1) * rows_half]

    def partial(h):
        low = jnp.dot(pooled_half[h], down_ref[...], preferred_element_type=f32)
        back = jnp.dot(weighted[h], up_ref[...], preferred_element_type=f32)
        return low.reshape(pairs, -1, rank), back.reshape(pairs, -1, rank)

    low, back = partial(1 - half)
    mate_out[:, :, :rank] = low.astype(bf16)
    mate_out[:, :, rank:] = back.astype(bf16)
    steps(pair_far + [0], lambda e: mate_copy(e).start())
    low, back = partial(half)
    own[:, :, :rank] = low
    own[:, :, rank:] = back

    def send_pair(e):
        mate_copy(e).wait_recv()
        pair_out[e] = (own[across(e)] + mate_in[e].astype(f32)).astype(bf16)
        pair_copy(e).start()

    steps(pair_far, send_pair)
    steps([0] + near, build_place)
    mate_copy(0).wait_recv()
    own[pair] = own[pair] + mate_in[0].astype(f32)

    def add_pair(e):
        pair_copy(e).wait_recv()
        own[pair] = own[pair] + pair_in[e].astype(f32)

    steps(pair_near, add_pair)
    full[half, pair] = own[pair].astype(bf16)
    steps(pair_far, lambda e: full_copy(e).start())
    pass_copy(half, 0).start()

    def pass_on(e):
        full_copy(e).wait_recv()
        pass_copy(half, e).start()

    steps(pair_near, pass_on)
    steps([0] + pair_near, lambda e: pass_copy(1 - half, e).wait_recv())

    low_half = full[:, :, :, :rank].reshape(samples, rank)
    back_half = full[:, :, :, rank:].reshape(samples, rank)
    transposed = (((1,), (1,)), ((), ()))
    left = lax.broadcasted_iota(jnp.int32, (samples, width), 1) < width // 2
    swap = lambda value: pltpu.roll(value, width // 2, 1)
    for f in range(features):
        cut = slice(f * width, (f + 1) * width)
        scaled = (
            lax.dot_general(low_half, up_ref[cut, :], transposed, preferred_element_type=f32)
            + bias_ref[:, cut]
        )
        wide = pooled_half[:, :, cut].reshape(samples, width).astype(f32)
        crossed_ref[:, cut] = (wide * scaled + wide).astype(bf16)
        upstream = cot_ref[:, cut].astype(f32)
        pool_grad = (
            upstream * scaled
            + upstream
            + lax.dot_general(back_half, down_ref[cut, :], transposed, preferred_element_type=f32)
        )
        value = (pool_grad / divisors[f]).astype(bf16).astype(f32)
        low_lanes = jnp.where(left, value, 0.0)
        high_lanes = jnp.where(left, 0.0, value)
        span = slice(f * samples, (f + 1) * samples)
        grad_half[0, 0, span, :] = low_lanes.astype(bf16)
        grad_half[0, 1, span, :] = swap(low_lanes).astype(bf16)
        grad_half[1, 0, span, :] = swap(high_lanes).astype(bf16)
        grad_half[1, 1, span, :] = high_lanes.astype(bf16)

    def packed_grads(h, d):
        return (
            jnp.dot(place[d, : cap // 2], grad_half[h, 0], preferred_element_type=f32)
            + jnp.dot(place[d, cap // 2 :], grad_half[h, 1], preferred_element_type=f32)
        ).astype(bf16)

    for h in range(2):

        def send_grads(d):
            grads_out[h, d] = packed_grads(h, d)
            grads_copy(h, d).start()

        steps(far, send_grads)
    for h in range(2):
        grads_in[h, 0] = packed_grads(h, 0)
    steps([0] + near, build_owned)

    def collect(h, d):
        value = grads_in[h, d].astype(f32)
        other = swap(value)
        first, second = (value, other) if h == 0 else (other, value)
        slots = jnp.concatenate([first, second], axis=0).astype(bf16)
        return jnp.dot(owned[d], slots, preferred_element_type=f32)

    share = rows // nr
    row_left = lax.broadcasted_iota(jnp.int32, (share // 2, width), 1) < width // 2

    def gather_half(h):
        row_sum[...] = collect(h, 0)

        def arrive(d):
            grads_copy(h, d).wait_recv()
            row_sum[...] += collect(h, d)

        steps(near, arrive)
        for q in range(nr):
            top = row_sum[q * share : q * share + share // 2, :]
            bottom = row_sum[q * share + share // 2 : (q + 1) * share, :]
            if h == 0:
                packed = jnp.where(row_left, top, swap(bottom))
            else:
                packed = jnp.where(row_left, swap(top), bottom)
            row_part[h, q] = packed.astype(bf16)
        steps(group_far, lambda e: row_part_copy(h, e).start())

    def reduce_half(h):
        row_total[...] = row_part[h, group].astype(f32)

        def arrive(e):
            row_part_copy(h, e).wait_recv()
            row_total[...] += row_part_in[h, e].astype(f32)

        steps(group_far[::-1], arrive)
        row_full[h, group] = row_total[...].astype(bf16)
        steps(group_far, lambda e: row_full_copy(h, e).start())

    gather_half(0)
    reduce_half(0)
    gather_half(1)
    reduce_half(1)
    for h in range(2):
        steps(group_far[::-1], lambda e: row_full_copy(h, e).wait_recv())
    for q in range(nr):
        first = row_full[0, q].astype(f32)
        second = row_full[1, q].astype(f32)
        top = jnp.where(row_left, first, swap(second))
        bottom = jnp.where(row_left, swap(first), second)
        grad_ref[q * share : q * share + share // 2, :] = top.astype(bf16)
        grad_ref[q * share + share // 2 : (q + 1) * share, :] = bottom.astype(bf16)

    steps(near, lambda d: rows_copy(d).wait_send())
    steps([0] + pair_near, lambda e: mate_copy(e).wait_send())
    steps(pair_near, lambda e: pair_copy(e).wait_send())
    steps(pair_near, lambda e: full_copy(e).wait_send())
    steps([0] + pair_near, lambda e: pass_copy(half, e).wait_send())
    for h in range(2):
        steps(near, lambda d: grads_copy(h, d).wait_send())
        steps(group_far, lambda e: row_part_copy(h, e).wait_send())
        steps(group_far, lambda e: row_full_copy(h, e).wait_send())


def shards(
    n,
    nr,
    row_table,
    grad_history,
    touched,
    lookup_slot,
    pool_counts,
    cross_down,
    cross_up,
    cross_bias,
    cotangent,
):
    rows, width = row_table.shape
    wanted = touched[0, 0]
    cap = wanted.shape[1]
    counts = pool_counts[0].T
    slots = lookup_slot[0].transpose(1, 2, 0)
    features, hot, samples = slots.shape
    rank = cross_down.shape[1]
    dma = pltpu.SemaphoreType.DMA
    vmem = pl.BlockSpec(memory_space=pltpu.VMEM)
    lookups = features * samples
    pieces = (n // 2, samples // n, 2 * rank)
    crossed, summed = pl.pallas_call(
        functools.partial(kernel, n, nr),
        out_shape=(
            jax.ShapeDtypeStruct((samples, features * width), bf16),
            jax.ShapeDtypeStruct((rows, width), bf16),
        ),
        in_specs=[vmem] * 8,
        out_specs=(vmem, vmem),
        scratch_shapes=[
            pltpu.VMEM((rows, width), bf16),
            pltpu.VMEM((cap, rows), bf16),
            pltpu.VMEM((n, cap, width), bf16),
            pltpu.VMEM((n, cap, width), bf16),
            pltpu.VMEM((hot * features, samples, LANES), jnp.int32),
            pltpu.VMEM((features, samples, width), f32),
            pltpu.VMEM((n, lookups, cap), bf16),
            pltpu.VMEM((n, cap, lookups), bf16),
            pltpu.VMEM((n, rows, cap), bf16),
            pltpu.VMEM((lookups, width), f32),
            pltpu.VMEM((2, samples // 2, features * width), bf16),
            pltpu.VMEM((2, samples // 2, features * width), bf16),
            pltpu.VMEM(pieces, bf16),
            pltpu.VMEM(pieces, bf16),
            pltpu.VMEM(pieces, f32),
            pltpu.VMEM(pieces, bf16),
            pltpu.VMEM(pieces, bf16),
            pltpu.VMEM((2, *pieces), bf16),
            pltpu.VMEM((2, 2, lookups, width), bf16),
            pltpu.VMEM((2, n, cap // 2, width), bf16),
            pltpu.VMEM((2, n, cap // 2, width), bf16),
            pltpu.VMEM((rows, width), f32),
            pltpu.VMEM((2, nr, rows // nr // 2, width), bf16),
            pltpu.VMEM((2, nr, rows // nr // 2, width), bf16),
            pltpu.VMEM((rows // nr // 2, width), f32),
            pltpu.VMEM((2, nr, rows // nr // 2, width), bf16),
        ]
        + [dma((n,))] * 2
        + [dma((2, n))] * 2
        + [dma((n // 2,))] * 8
        + [dma((2, nr))] * 4,
        compiler_params=pltpu.CompilerParams(
            collective_id=0, has_side_effects=True, vmem_limit_bytes=56 * 1024 * 1024
        ),
        cost_estimate=pl.CostEstimate(flops=10**9 * 6, bytes_accessed=10**7, transcendentals=0),
    )(row_table, wanted, slots, counts, cross_down, cross_up, cross_bias[None, :], cotangent[0])
    summed = summed.astype(f32)
    fresh_history_sums = grad_history + summed * summed
    new_table = row_table - learn_rate * summed / (jnp.sqrt(fresh_history_sums) + epsilon)
    return (crossed[None], new_table, fresh_history_sums)


def solution(mesh):
    in_specs = (
        P("mp", None),
        P("mp", None),
        P("replica", "mp", None, None),
        P("replica", None, "mp", None),
        P("replica", None, "mp"),
        P("mp", None),
        P("mp", None),
        P("mp"),
        P("replica", None, "mp"),
    )
    out_specs = (P("replica", None, "mp"), P("mp", None), P("mp", None))
    body = functools.partial(shards, mesh.shape["mp"], mesh.shape["replica"])
    return jax.shard_map(body, mesh=mesh, in_specs=in_specs, out_specs=out_specs, check_vma=False)
```

```python
import functools

import jax
import jax.numpy as jnp
from jax import lax
from jax.experimental import pallas as pl
from jax.experimental.pallas import tpu as pltpu
from jax.sharding import PartitionSpec as P

learn_rate = 0.5
epsilon = 1e-06
LANES = 128
bf16 = jnp.bfloat16
f32 = jnp.float32


def flip(index, distance, count):
    result = 0
    bit = 1
    while bit < count:
        result = result + bit * lax.rem(
            lax.div(jnp.int32(index), jnp.int32(bit)) + lax.div(jnp.int32(distance), jnp.int32(bit)),
            jnp.int32(2),
        )
        bit *= 2
    return result


def steps(order, body):
    if len(order) <= 8:
        for d in order:
            body(d)
    else:
        first, stride = order[0], order[1] - order[0]
        lax.fori_loop(0, len(order), lambda i, c: (body(first + stride * i), c)[1], 0)


def ones_where(mask):
    return jnp.where(mask, 1.0, 0.0).astype(bf16)


def kernel(
    n,
    nr,
    table_ref,
    wanted_ref,
    slots_ref,
    counts_ref,
    down_ref,
    up_ref,
    bias_ref,
    cot_ref,
    crossed_ref,
    grad_ref,
    table_half,
    onehot,
    rows_out,
    rows_in,
    columns,
    divisors,
    pick,
    place,
    owned,
    pool_sum,
    pooled_half,
    weighted,
    mate_out,
    mate_in,
    own,
    pair_out,
    pair_in,
    full,
    grad_half,
    grads_out,
    grads_in,
    row_sum,
    row_part,
    row_part_in,
    row_reduced,
    row_full,
    rows_send,
    rows_recv,
    grads_send,
    grads_recv,
    mate_send,
    mate_recv,
    pair_send,
    pair_recv,
    full_send,
    full_recv,
    pass_send,
    pass_recv,
    row_part_send,
    row_part_recv,
    row_full_send,
    row_full_recv,
):
    me = lax.axis_index("mp")
    group = lax.axis_index("replica")
    cap = wanted_ref.shape[1]
    rows, width = table_ref.shape
    features, hot, samples = slots_ref.shape
    rank = down_ref.shape[1]
    piece = min(cap, LANES)
    near = list(range(1, n))
    far = near[::-1]
    group_far = list(range(nr - 1, 0, -1))

    barrier = pltpu.get_barrier_semaphore()
    for_mp = lambda d: pl.semaphore_signal(
        barrier, inc=1, device_id={"mp": flip(me, d, n)}, device_id_type=pl.DeviceIdType.MESH
    )
    for_replica = lambda e: pl.semaphore_signal(
        barrier, inc=1, device_id={"replica": flip(group, e, nr)}, device_id_type=pl.DeviceIdType.MESH
    )
    steps(far, for_mp)
    steps(group_far, for_replica)

    def to_mp(src, dst, send, recv, d):
        return pltpu.make_async_remote_copy(
            src_ref=src,
            dst_ref=dst,
            send_sem=send.at[d],
            recv_sem=recv.at[d],
            device_id={"mp": flip(me, d, n)},
            device_id_type=pl.DeviceIdType.MESH,
        )

    def to_replica(src, dst, send, recv, e):
        return pltpu.make_async_remote_copy(
            src_ref=src,
            dst_ref=dst,
            send_sem=send.at[e],
            recv_sem=recv.at[e],
            device_id={"replica": flip(group, e, nr)},
            device_id_type=pl.DeviceIdType.MESH,
        )

    rows_copy = lambda d: to_mp(rows_out.at[d], rows_in.at[d], rows_send, rows_recv, d)
    grads_copy = lambda d: to_mp(grads_out.at[d], grads_in.at[d], grads_send, grads_recv, d)
    row_part_copy = lambda e: to_replica(
        row_part.at[flip(group, e, nr)], row_part_in.at[e], row_part_send, row_part_recv, e
    )
    row_full_copy = lambda e: to_replica(
        row_reduced, row_full.at[group], row_full_send, row_full_recv, e
    )

    pairs = n // 2
    half = lax.rem(me, jnp.int32(2))
    pair = lax.div(me, jnp.int32(2))
    mate = me + 1 - 2 * half
    pair_near = list(range(1, pairs))
    pair_far = pair_near[::-1]

    def to_device(src, dst, send, recv, device):
        return pltpu.make_async_remote_copy(
            src_ref=src,
            dst_ref=dst,
            send_sem=send,
            recv_sem=recv,
            device_id={"mp": device},
            device_id_type=pl.DeviceIdType.MESH,
        )

    across = lambda e: flip(pair, e, pairs)
    mate_copy = lambda e: to_device(
        mate_out.at[across(e)], mate_in.at[e], mate_send.at[e], mate_recv.at[e], mate
    )
    pair_copy = lambda e: to_device(
        pair_out.at[e], pair_in.at[e], pair_send.at[e], pair_recv.at[e], 2 * across(e) + half
    )
    full_copy = lambda e: to_device(
        full.at[half, pair],
        full.at[half, pair],
        full_send.at[e],
        full_recv.at[e],
        2 * across(e) + half,
    )
    pass_copy = lambda h, e: to_device(
        full.at[h, across(e)], full.at[h, across(e)], pass_send.at[e], pass_recv.at[e], mate
    )

    table_half[...] = table_ref[...].astype(bf16)
    lane = lax.broadcasted_iota(jnp.int32, (cap, LANES), 1)

    def gather(d):
        row = wanted_ref[pl.ds(flip(me, d, n), 1), :]
        column = jnp.broadcast_to(row, (LANES, cap)).T
        for j in range(rows // LANES):
            onehot[:, j * LANES : (j + 1) * LANES] = ones_where(column == lane + j * LANES)
        return jnp.dot(onehot[...], table_half[...], preferred_element_type=f32).astype(bf16)

    rows_out[n - 1] = gather(n - 1)
    pl.semaphore_wait(barrier, n - 1 + nr - 1)
    rows_copy(n - 1).start()

    def send_rows(d):
        rows_out[d] = gather(d)
        rows_copy(d).start()

    steps(far[1:], send_rows)
    rows_in[0] = gather(0)

    slot_rows = {}
    for f in range(features):
        count = counts_ref[f : f + 1, :]
        divisors[f] = jnp.broadcast_to(count.astype(f32), (width, samples)).T
        for k in range(hot):
            row = jnp.where(k < count, slots_ref[f, k : k + 1, :], -1)
            slot_rows[f, k] = row
            columns[k * features + f] = jnp.broadcast_to(row, (LANES, samples)).T
    piece_lane = lax.broadcasted_iota(jnp.int32, (samples, piece), 1)
    cap_row = lax.broadcasted_iota(jnp.int32, (cap, samples), 0)
    block_row = lax.broadcasted_iota(jnp.int32, (LANES, cap), 0)

    def build_pick(d):
        base = flip(me, d, n) * cap
        for f in range(features):
            for j in range(cap // piece):
                mask = None
                for k in range(hot):
                    hit = columns[k * features + f][:, :piece] - (base + j * piece) == piece_lane
                    mask = hit if mask is None else mask | hit
                pick[d, f * samples : (f + 1) * samples, j * piece : (j + 1) * piece] = ones_where(mask)

    def build_place(d):
        base = flip(me, d, n) * cap
        for f in range(features):
            mask = None
            for k in range(hot):
                hit = slot_rows[f, k] - base == cap_row
                mask = hit if mask is None else mask | hit
            place[d, :, f * samples : (f + 1) * samples] = ones_where(mask)

    def build_owned(d):
        row = wanted_ref[pl.ds(flip(me, d, n), 1), :]
        for j in range(rows // LANES):
            owned[d, j * LANES : (j + 1) * LANES, :] = ones_where(row == block_row + j * LANES)

    steps([0] + near, build_pick)
    pool_sum[...] = jnp.dot(pick[0], rows_in[0], preferred_element_type=f32)

    def pool(d):
        rows_copy(d).wait_recv()
        pool_sum[...] += jnp.dot(pick[d], rows_in[d], preferred_element_type=f32)

    steps(near, pool)

    rows_half = samples // 2
    for f in range(features):
        cut = slice(f * width, (f + 1) * width)
        value = (pool_sum[f * samples : (f + 1) * samples, :] / divisors[f]).astype(bf16)
        change = (cot_ref[:, cut].astype(f32) * value.astype(f32)).astype(bf16)
        for h in range(2):
            pooled_half[h, :, cut] = value[h * rows_half : (h + 1) * rows_half]
            weighted[h, :, cut] = change[h * rows_half : (h + 1) * rows_half]

    def partial(h):
        low = jnp.dot(pooled_half[h], down_ref[...], preferred_element_type=f32)
        back = jnp.dot(weighted[h], up_ref[...], preferred_element_type=f32)
        return low.reshape(pairs, -1, rank), back.reshape(pairs, -1, rank)

    low, back = partial(1 - half)
    mate_out[:, :, :rank] = low.astype(bf16)
    mate_out[:, :, rank:] = back.astype(bf16)
    steps(pair_far + [0], lambda e: mate_copy(e).start())
    low, back = partial(half)
    own[:, :, :rank] = low
    own[:, :, rank:] = back

    def send_pair(e):
        mate_copy(e).wait_recv()
        pair_out[e] = (own[across(e)] + mate_in[e].astype(f32)).astype(bf16)
        pair_copy(e).start()

    steps(pair_far, send_pair)
    steps([0] + near, build_place)
    mate_copy(0).wait_recv()
    own[pair] = own[pair] + mate_in[0].astype(f32)

    def add_pair(e):
        pair_copy(e).wait_recv()
        own[pair] = own[pair] + pair_in[e].astype(f32)

    steps(pair_near, add_pair)
    full[half, pair] = own[pair].astype(bf16)
    steps(pair_far, lambda e: full_copy(e).start())
    pass_copy(half, 0).start()

    def pass_on(e):
        full_copy(e).wait_recv()
        pass_copy(half, e).start()

    steps(pair_near, pass_on)
    steps([0] + pair_near, lambda e: pass_copy(1 - half, e).wait_recv())

    low_half = full[:, :, :, :rank].reshape(samples, rank)
    back_half = full[:, :, :, rank:].reshape(samples, rank)
    transposed = (((1,), (1,)), ((), ()))
    for f in range(features):
        cut = slice(f * width, (f + 1) * width)
        scaled = (
            lax.dot_general(low_half, up_ref[cut, :], transposed, preferred_element_type=f32)
            + bias_ref[:, cut]
        )
        wide = pooled_half[:, :, cut].reshape(samples, width).astype(f32)
        crossed_ref[:, cut] = (wide * scaled + wide).astype(bf16)
        upstream = cot_ref[:, cut].astype(f32)
        pool_grad = (
            upstream * scaled
            + upstream
            + lax.dot_general(back_half, down_ref[cut, :], transposed, preferred_element_type=f32)
        )
        grad_half[f * samples : (f + 1) * samples, :] = (pool_grad / divisors[f]).astype(bf16)

    def send_grads(d):
        grads_out[d] = jnp.dot(place[d], grad_half[...], preferred_element_type=f32).astype(bf16)
        grads_copy(d).start()

    steps(far, send_grads)
    steps([0] + near, build_owned)
    grads_in[0] = jnp.dot(place[0], grad_half[...], preferred_element_type=f32).astype(bf16)
    row_sum[...] = jnp.dot(owned[0], grads_in[0], preferred_element_type=f32)

    def collect(d):
        grads_copy(d).wait_recv()
        row_sum[...] += jnp.dot(owned[d], grads_in[d], preferred_element_type=f32)

    steps(near, collect)

    row_part[...] = row_sum[...].reshape(row_part.shape).astype(bf16)
    steps(group_far, lambda e: row_part_copy(e).start())
    total = row_part[group].astype(f32)
    if nr <= 8:
        for e in group_far[::-1]:
            row_part_copy(e).wait_recv()
            total = total + row_part_in[e].astype(f32)
    else:

        def add_rows(i, value):
            row_part_copy(i + 1).wait_recv()
            return value + row_part_in[i + 1].astype(f32)

        total = lax.fori_loop(0, nr - 1, add_rows, total)
    row_reduced[...] = total.astype(bf16)
    steps(group_far, lambda e: row_full_copy(e).start())
    row_full[group] = row_reduced[...]
    steps(group_far[::-1], lambda e: row_full_copy(e).wait_recv())
    grad_ref[...] = row_full[...].reshape(rows, width)

    steps(near, lambda d: rows_copy(d).wait_send())
    steps([0] + pair_near, lambda e: mate_copy(e).wait_send())
    steps(pair_near, lambda e: pair_copy(e).wait_send())
    steps(pair_near, lambda e: full_copy(e).wait_send())
    steps([0] + pair_near, lambda e: pass_copy(half, e).wait_send())
    steps(near, lambda d: grads_copy(d).wait_send())
    steps(group_far, lambda e: row_part_copy(e).wait_send())
    steps(group_far, lambda e: row_full_copy(e).wait_send())


def shards(
    n,
    nr,
    row_table,
    grad_history,
    touched,
    lookup_slot,
    pool_counts,
    cross_down,
    cross_up,
    cross_bias,
    cotangent,
):
    rows, width = row_table.shape
    wanted = touched[0, 0]
    cap = wanted.shape[1]
    counts = pool_counts[0].T
    slots = lookup_slot[0].transpose(1, 2, 0)
    features, hot, samples = slots.shape
    rank = cross_down.shape[1]
    dma = pltpu.SemaphoreType.DMA
    vmem = pl.BlockSpec(memory_space=pltpu.VMEM)
    lookups = features * samples
    pieces = (n // 2, samples // n, 2 * rank)
    crossed, summed = pl.pallas_call(
        functools.partial(kernel, n, nr),
        out_shape=(
            jax.ShapeDtypeStruct((samples, features * width), bf16),
            jax.ShapeDtypeStruct((rows, width), bf16),
        ),
        in_specs=[vmem] * 8,
        out_specs=(vmem, vmem),
        scratch_shapes=[
            pltpu.VMEM((rows, width), bf16),
            pltpu.VMEM((cap, rows), bf16),
            pltpu.VMEM((n, cap, width), bf16),
            pltpu.VMEM((n, cap, width), bf16),
            pltpu.VMEM((hot * features, samples, LANES), jnp.int32),
            pltpu.VMEM((features, samples, width), f32),
            pltpu.VMEM((n, lookups, cap), bf16),
            pltpu.VMEM((n, cap, lookups), bf16),
            pltpu.VMEM((n, rows, cap), bf16),
            pltpu.VMEM((lookups, width), f32),
            pltpu.VMEM((2, samples // 2, features * width), bf16),
            pltpu.VMEM((2, samples // 2, features * width), bf16),
            pltpu.VMEM(pieces, bf16),
            pltpu.VMEM(pieces, bf16),
            pltpu.VMEM(pieces, f32),
            pltpu.VMEM(pieces, bf16),
            pltpu.VMEM(pieces, bf16),
            pltpu.VMEM((2, *pieces), bf16),
            pltpu.VMEM((lookups, width), bf16),
            pltpu.VMEM((n, cap, width), bf16),
            pltpu.VMEM((n, cap, width), bf16),
            pltpu.VMEM((rows, width), f32),
            pltpu.VMEM((nr, rows // nr, width), bf16),
            pltpu.VMEM((nr, rows // nr, width), bf16),
            pltpu.VMEM((rows // nr, width), bf16),
            pltpu.VMEM((nr, rows // nr, width), bf16),
        ]
        + [dma((n,))] * 4
        + [dma((n // 2,))] * 8
        + [dma((nr,))] * 4,
        compiler_params=pltpu.CompilerParams(
            collective_id=0, has_side_effects=True, vmem_limit_bytes=56 * 1024 * 1024
        ),
        cost_estimate=pl.CostEstimate(flops=10**9 * 6, bytes_accessed=10**7, transcendentals=0),
    )(row_table, wanted, slots, counts, cross_down, cross_up, cross_bias[None, :], cotangent[0])
    summed = summed.astype(f32)
    fresh_history_sums = grad_history + summed * summed
    new_table = row_table - learn_rate * summed / (jnp.sqrt(fresh_history_sums) + epsilon)
    return (crossed[None], new_table, fresh_history_sums)


def solution(mesh):
    in_specs = (
        P("mp", None),
        P("mp", None),
        P("replica", "mp", None, None),
        P("replica", None, "mp", None),
        P("replica", None, "mp"),
        P("mp", None),
        P("mp", None),
        P("mp"),
        P("replica", None, "mp"),
    )
    out_specs = (P("replica", None, "mp"), P("mp", None), P("mp", None))
    body = functools.partial(shards, mesh.shape["mp"], mesh.shape["replica"])
    return jax.shard_map(body, mesh=mesh, in_specs=in_specs, out_specs=out_specs, check_vma=False)
```
